32 devices in a mesh: section: 2 (over x), space: 16 (over z, y, core).
Axes of the slice: x: 2, y: 2, z: 4, core: 2. Of those that a mesh axis runs over, the one named last changes fastest.
Arguments:
- acts: bfloat16 [2, 2, 2048, 1024], P('section', None, 'space'), may hold values from -6 to 6
- upstream: bfloat16 [2, 2048, 1024], P(None, 'space'), may hold values from -4 to 4
- weights: bfloat16 [2, 1024, 1024], P('section'), may hold values from -0.1875 to 0.1875
- neighbours: int32 [2048, 6], P('space'), may hold values from 0 to 2047, as said below
Outputs:
- input_grads: bfloat16 [2, 2, 2048, 1024], P('section', None, 'space')
- weight_grads: float32 [2, 1024, 1024], P('section', 'space')
The draws below stay inside these ranges and needn't reach their ends.
Inputs may be any that keep to these rules, and one draw needn't show every extreme that they name: neighbours[i, k] is a node at most 32 positions from node i along the node order, taken cyclically over all 2048 nodes; the distance 32 is reached on both sides.
All inputs are finite; a program needn't handle non-finite values.
Results may differ from the reference program's by a relative error of at most 0.014.
Values may be sent and summed in bfloat16 or wider, within the bound.
A program may use at most 64 MiB of HBM per device.

```python
import jax
import jax.numpy as jnp
from jax import lax

D = 1024
K = 6
HALO = 32
M = 2
SECTIONS = 2
NODES = 2048


def draw_neighbours(key, part):
    offsets = jax.random.randint(key, (NODES, K), -HALO, HALO + 1)
    offsets = offsets.at[0, 0].set(HALO).at[1, 0].set(-HALO)
    base = jnp.arange(NODES, dtype=jnp.int32)[:, None]
    return jnp.mod(base + offsets, NODES).astype(jnp.int32)


def shard_levels(key, dims, split, smallest, largest):
    factor_of = 1.0
    for dim, blocks in split:
        draws = jax.random.uniform(jax.random.fold_in(jax.random.fold_in(key, 6), dim), (blocks,), jnp.float32, smallest / len(split), largest / len(split))
        factor_of = factor_of * jnp.repeat(jnp.exp(draws), dims[dim] // blocks).reshape((-1,) + (1,) * (len(dims) - 1 - dim))
    return factor_of


def bell_draw(rng, dims, width, limit, shards=(), held_as=jnp.bfloat16):
    loudness = shard_levels(rng, dims, shards, -0.22, 0.18) if shards else 1.0
    values = jax.random.normal(rng, dims, jnp.float32) * width * loudness
    return jnp.minimum(jnp.maximum(values, -limit), limit).astype(held_as)


def setup_inputs(seed: int = 0) -> dict:
    seeds = jax.random.split(jax.random.key(seed), 5)
    acts = bell_draw(seeds[0], (SECTIONS, M, NODES, D), 1.0, 6.0, ((0, 2), (2, 16)))
    upstream = bell_draw(seeds[1], (M, NODES, D), 0.5, 4.0, ((1, 16),))
    weights = bell_draw(seeds[2], (SECTIONS, D, D), D ** -0.5, 0.1875, ((0, 2),))
    neighbours = draw_neighbours(jax.random.fold_in(seeds[4], 71), 0)
    return dict(acts=acts, upstream=upstream, weights=weights, neighbours=neighbours)


def layer_back(h_field, g_field, weight, neighbours):
    agg = jnp.mean(h_field[neighbours].astype(jnp.float32), axis=1)
    z_field = (h_field.astype(jnp.float32) + agg).astype(jnp.bfloat16)
    u_field = jnp.dot(z_field, weight, preferred_element_type=jnp.float32)
    sig = jax.nn.sigmoid(u_field)
    du_field = (g_field.astype(jnp.float32) * sig * (1.0 + u_field * (1.0 - sig))).astype(jnp.bfloat16)
    dz_field = lax.dot_general(du_field, weight, (((1,), (1,)), ((), ())), preferred_element_type=jnp.float32)
    share = dz_field * (1.0 / K)
    spread = jnp.zeros(dz_field.shape, jnp.float32).at[neighbours.reshape(-1)].add(
        jnp.broadcast_to(share[:, None, :], (share.shape[0], K, share.shape[1])).reshape(-1, share.shape[1]))
    d_input = (g_field.astype(jnp.float32) + dz_field + spread).astype(jnp.bfloat16)
    d_weight = lax.dot_general(z_field, du_field, (((0,), (0,)), ((), ())), preferred_element_type=jnp.float32)
    return d_input, d_weight


def reference(acts, upstream, weights, neighbours):
    grads = [None] * SECTIONS
    wgrads = [None] * SECTIONS
    carried = [upstream[m] for m in range(M)]
    for section in reversed(range(SECTIONS)):
        total = jnp.zeros((D, D), jnp.float32)
        outs = []
        for m in range(M):
            d_input, d_weight = layer_back(acts[section, m], carried[m], weights[section], neighbours)
            outs.append(d_input)
            total = total + d_weight
        carried = outs
        grads[section] = jnp.stack(outs)
        wgrads[section] = total
    return jnp.stack(grads), jnp.stack(wgrads)
```

```python
import functools

import jax
import jax.numpy as jnp
from jax import lax
from jax.experimental import pallas as pl
from jax.experimental.pallas import tpu as pltpu
from jax.sharding import PartitionSpec as P

K = 6
HALO = 32
CHUNK = 256
MESH = pl.DeviceIdType.MESH
F32 = jnp.float32
BF16 = jnp.bfloat16


def radices_of(count):
    found = []
    for _ in range(2):
        if count % 2 == 0:
            found.append(2)
            count //= 2
    while count > 1:
        factor = next(f for f in (2, 3, 5, 7, count) if count % f == 0)
        found.append(factor)
        count //= factor
    return tuple(found)


def position(piece, radices):
    left = 1
    for r in radices:
        left *= r
    place = 0
    for r in radices:
        left //= r
        place += (piece % r) * left
        piece //= r
    return place


def kernel(sections, count, radices, chunk, nbr, acts, ups_hbm, w_hbm, out, wgrad, *scratch):
    (w, ups, acts_lo, acts_hi, nbr_lo, nbr_hi, z, zt, fac, g_in, g_out, du, du_lo, du_hi, e,
     load_sem, acts_send, acts_recv, nbr_send, nbr_recv, g_send, g_recv, du_send, du_recv,
     rs_send, rs_recv, *rs) = scratch
    stages = len(radices)
    parts, landed = rs[:stages], rs[stages:]
    micro, rows, width = acts.shape
    chunks = width // chunk
    span = rows + 2 * HALO
    s = lax.axis_index("section")
    me = lax.axis_index("space")
    right, left = lax.rem(me + 1, count), lax.rem(me + count - 1, count)
    top = s == sections - 1

    strides, digits, stride = [], [], 1
    for r in radices:
        strides.append(stride)
        digits.append(lax.rem(lax.div(me, stride), r))
        stride *= r

    def peer(t, j):
        digit = lax.rem(digits[t] + j, radices[t])
        return digit, me + (digit - digits[t]) * strides[t]

    loads = [pltpu.make_async_copy(w_hbm, w, load_sem.at[0]),
             pltpu.make_async_copy(ups_hbm, ups, load_sem.at[1])]
    for copy in loads:
        copy.start()

    barrier = pltpu.get_barrier_semaphore()
    partners = [left, right] + [peer(t, j)[1] for t in range(stages) for j in range(1, radices[t])]
    for partner in partners:
        pl.semaphore_signal(barrier, inc=1, device_id=(s, partner), device_id_type=MESH)

    @pl.when(s > 0)
    def _():
        pl.semaphore_signal(barrier, inc=1, device_id=(s - 1, me), device_id_type=MESH)

    @pl.when(s < sections - 1)
    def _():
        pl.semaphore_signal(barrier, inc=1, device_id=(s + 1, me), device_id_type=MESH)

    layers = jnp.where(s > 0, 1, 0) + jnp.where(s < sections - 1, 1, 0)
    pl.semaphore_wait(barrier, len(partners) + layers)

    def remote(src, dst, send, recv, where):
        return pltpu.make_async_remote_copy(
            src_ref=src, dst_ref=dst, send_sem=send, recv_sem=recv, device_id=where,
            device_id_type=MESH)

    first, last = pl.ds(0, HALO), pl.ds(rows - HALO, HALO)
    halos = [
        remote(acts.at[:, last], acts_lo, acts_send.at[0], acts_recv.at[0], (s, right)),
        remote(acts.at[:, first], acts_hi, acts_send.at[1], acts_recv.at[1], (s, left)),
        remote(nbr.at[last], nbr_lo, nbr_send.at[0], nbr_recv.at[0], (s, right)),
        remote(nbr.at[first], nbr_hi, nbr_send.at[1], nbr_recv.at[1], (s, left)),
    ]
    for copy in halos:
        copy.start()

    total = rows * count

    def counts(ids, shift, lanes):
        local = ids - me * rows + shift
        local = jnp.where(local < 0, local + total, local)
        local = jnp.where(local >= total, local - total, local)
        places = lax.broadcasted_iota(jnp.int32, (ids.shape[0], lanes), 1)
        found = jnp.zeros(places.shape, F32)
        for k in range(K):
            found = found + jnp.where(local[:, k:k + 1] == places, 1.0, 0.0)
        return found.astype(BF16)

    gather = counts(nbr[...], HALO, span)
    own = counts(nbr[...], 0, rows)

    for copy in halos:
        copy.wait_recv()
    scatter = jnp.concatenate(
        [counts(nbr_lo[...], 0, rows), own, counts(nbr_hi[...], 0, rows)], axis=0
    ).astype(F32).T.astype(BF16)

    for m in range(micro):
        field = jnp.concatenate([acts_lo[m], acts[m], acts_hi[m]], axis=0)
        agg = jnp.dot(gather, field, preferred_element_type=F32) * (1.0 / K)
        z[m * rows:(m + 1) * rows] = (acts[m].astype(F32) + agg).astype(BF16)
    for copy in loads:
        copy.wait()

    def columns(c):
        return slice(c * chunk, (c + 1) * chunk)

    def factor(c):
        u = jnp.dot(z[...], w[:, columns(c)], preferred_element_type=F32)
        sig = jax.nn.sigmoid(u)
        return sig * (1.0 + u * (1.0 - sig))

    def turn():
        zt[...] = z[...].astype(F32).T.astype(BF16)

    def du_copies(c):
        return [
            remote(du.at[c, :, last], du_lo.at[c], du_send.at[2 * c], du_recv.at[2 * c], (s, right)),
            remote(du.at[c, :, first], du_hi.at[c], du_send.at[2 * c + 1], du_recv.at[2 * c + 1],
                   (s, left)),
        ]

    def put_du(c, value):
        value = value.astype(BF16)
        du[c] = value.reshape(micro, rows, chunk)
        for copy in du_copies(c):
            copy.start()

    def mix(c):
        for copy in du_copies(c):
            copy.wait_recv()
        for m in range(micro):
            field = jnp.concatenate([du_lo[c, m], du[c, m], du_hi[c, m]], axis=0)
            spread = jnp.dot(scatter, field, preferred_element_type=F32) * (1.0 / K)
            e[m * rows:(m + 1) * rows, columns(c)] = (du[c, m].astype(F32) + spread).astype(BF16)

    def cotangent(c, g):
        value = g.astype(F32) + lax.dot_general(
            e[...], w[columns(c), :], (((1,), (1,)), ((), ())), preferred_element_type=F32)
        value = value.astype(BF16)
        out[:, columns(c)] = value
        return value

    def rs_copies(t, c):
        groups = parts[t].shape[1] // radices[t]
        base = sum(r - 1 for r in radices[:t]) * chunks + c * (radices[t] - 1)
        made = []
        for j in range(1, radices[t]):
            digit, partner = peer(t, j)
            made.append(remote(
                parts[t].at[c, pl.ds(digit * groups, groups)], landed[t].at[c, j - 1],
                rs_send.at[base + j - 1], rs_recv.at[base + j - 1], (s, partner)))
        return made

    def rs_start(t, c):
        for copy in rs_copies(t, c):
            copy.start()

    def weight_part(c):
        found = jnp.dot(zt[...], du[c].reshape(micro * rows, chunk), preferred_element_type=F32)
        found = found.astype(BF16)
        deep = width // count
        for piece in range(count):
            parts[0][c, position(piece, radices)] = found[piece * deep:(piece + 1) * deep]
        rs_start(0, c)

    def rs_step(t, c):
        for copy in rs_copies(t, c):
            copy.wait_recv()
        groups = parts[t].shape[1] // radices[t]
        value = parts[t][c, pl.ds(digits[t] * groups, groups)].astype(F32)
        for j in range(radices[t] - 1):
            value = value + landed[t][c, j].astype(F32)
        if t == stages - 1:
            wgrad[:, columns(c)] = value[0]
        else:
            parts[t + 1][c] = value.astype(BF16)
            rs_start(t + 1, c)

    def rs_wave(step):
        for t in reversed(range(stages)):
            if 0 <= step - t < chunks:
                rs_step(t, step - t)

    def g_copy(c):
        return remote(g_out.at[c], g_in.at[c], g_send.at[c], g_recv.at[c], (s - 1, me))

    @pl.when(top)
    def _():
        for c in range(chunks):
            put_du(c, ups[:, columns(c)].astype(F32) * factor(c))
        turn()
        for c in range(chunks):
            weight_part(c)
        for c in range(chunks):
            mix(c)
        for c in range(chunks):
            g_out[c] = cotangent(c, ups[:, columns(c)])
            if sections > 1:
                g_copy(c).start()
        for step in range(chunks + stages - 1):
            rs_wave(step)
        if sections > 1:
            for c in range(chunks):
                g_copy(c).wait_send()

    if sections > 1:
        @pl.when(jnp.logical_not(top))
        def _():
            for c in range(chunks):
                fac[:, columns(c)] = factor(c)
            turn()
            for c in range(chunks):
                g_copy(c).wait_recv()
                put_du(c, g_in[c].astype(F32) * fac[:, columns(c)])
                weight_part(c)
                if c:
                    rs_wave(c - 1)
            rs_wave(chunks - 1)
            for c in range(chunks):
                mix(c)
            for c in range(chunks):
                g_out[c] = cotangent(c, g_in[c])

                @pl.when(s > 0)
                def _():
                    g_copy(c).start()
            for step in range(chunks, chunks + stages - 1):
                rs_wave(step)

            @pl.when(s > 0)
            def _():
                for c in range(chunks):
                    g_copy(c).wait_send()

    for copy in halos:
        copy.wait_send()
    for c in range(chunks):
        for copy in du_copies(c):
            copy.wait_send()
        for t in range(stages):
            for copy in rs_copies(t, c):
                copy.wait_send()


def shards(sections, count, acts, upstream, weights, neighbours):
    micro, rows, width = upstream.shape
    chunk = min(CHUNK, width)
    chunks = width // chunk
    radices = radices_of(count)
    held, parts, landed = count, [], []
    deep = width // count
    for r in radices:
        parts.append(pltpu.VMEM((chunks, held, deep, chunk), BF16))
        held //= r
        landed.append(pltpu.VMEM((chunks, r - 1, held, deep, chunk), BF16))
    flights = sum(r - 1 for r in radices) * chunks
    dma = pltpu.SemaphoreType.DMA
    tall = micro * rows
    scratch = [
        pltpu.VMEM((width, width), BF16),
        pltpu.VMEM((tall, width), BF16),
        pltpu.VMEM((micro, HALO, width), BF16),
        pltpu.VMEM((micro, HALO, width), BF16),
        pltpu.VMEM((HALO, K), jnp.int32),
        pltpu.VMEM((HALO, K), jnp.int32),
        pltpu.VMEM((tall, width), BF16),
        pltpu.VMEM((width, tall), BF16),
        pltpu.VMEM((tall, width), F32),
        pltpu.VMEM((chunks, tall, chunk), BF16),
        pltpu.VMEM((chunks, tall, chunk), BF16),
        pltpu.VMEM((chunks, micro, rows, chunk), BF16),
        pltpu.VMEM((chunks, micro, HALO, chunk), BF16),
        pltpu.VMEM((chunks, micro, HALO, chunk), BF16),
        pltpu.VMEM((tall, width), BF16),
        dma((2,)), dma((2,)), dma((2,)), dma((2,)), dma((2,)), dma((chunks,)), dma((chunks,)),
        dma((2 * chunks,)), dma((2 * chunks,)), dma((flights,)), dma((flights,)),
    ] + parts + landed
    vmem = pl.BlockSpec(memory_space=pltpu.VMEM)
    grads, weight_grad = pl.pallas_call(
        functools.partial(kernel, sections, count, radices, chunk),
        out_shape=(
            jax.ShapeDtypeStruct((tall, width), BF16),
            jax.ShapeDtypeStruct((deep, width), F32),
        ),
        in_specs=[vmem, vmem, pl.BlockSpec(memory_space=pl.ANY), pl.BlockSpec(memory_space=pl.ANY)],
        out_specs=(vmem, vmem),
        scratch_shapes=scratch,
        compiler_params=pltpu.CompilerParams(
            collective_id=0, has_side_effects=True, vmem_limit_bytes=48 * 1024 * 1024),
    )(neighbours, acts[0], upstream.reshape(tall, width), weights[0])
    return grads.reshape(1, micro, rows, width), weight_grad[None]


def solution(mesh):
    in_specs = (
        P("section", None, "space", None),
        P(None, "space", None),
        P("section", None, None),
        P("space", None),
    )
    out_specs = (P("section", None, "space", None), P("section", "space", None))
    body = functools.partial(shards, mesh.shape["section"], mesh.shape["space"])
    return jax.shard_map(
        body, mesh=mesh, in_specs=in_specs, out_specs=out_specs, check_vma=False)
```

```python
import functools

import jax
import jax.numpy as jnp
from jax import lax
from jax.experimental import pallas as pl
from jax.experimental.pallas import tpu as pltpu
from jax.sharding import PartitionSpec as P

K = 6
HALO = 32
CHUNK = 256
MESH = pl.DeviceIdType.MESH
F32 = jnp.float32
BF16 = jnp.bfloat16


def radices_of(count):
    found = []
    for _ in range(2):
        if count % 2 == 0:
            found.append(2)
            count //= 2
    while count > 1:
        factor = next(f for f in (4, 2, 3, 5, 7, count) if count % f == 0)
        found.append(factor)
        count //= factor
    return tuple(found)


def position(piece, radices):
    left = 1
    for r in radices:
        left *= r
    place = 0
    for r in radices:
        left //= r
        place += (piece % r) * left
        piece //= r
    return place


def kernel(sections, count, radices, chunk, nbr, acts_hbm, ups_hbm, w_hbm, out, wgrad, *scratch):
    (w, ups, acts, acts_lo, acts_hi, nbr_lo, nbr_hi, z, zt, fac, g_in, g_out, du, du_lo, du_hi, e,
     load_sem, acts_send, acts_recv, nbr_send, nbr_recv, g_send, g_recv, du_send, du_recv,
     rs_send, rs_recv, *rs) = scratch
    stages = len(radices)
    parts, landed = rs[:stages], rs[stages:]
    micro, rows, width = acts.shape
    chunks = width // chunk
    span = rows + 2 * HALO
    s = lax.axis_index("section")
    me = lax.axis_index("space")
    right, left = lax.rem(me + 1, count), lax.rem(me + count - 1, count)
    top = s == sections - 1

    strides, digits, stride = [], [], 1
    for r in radices:
        strides.append(stride)
        digits.append(lax.rem(lax.div(me, stride), r))
        stride *= r

    def peer(t, j):
        digit = lax.rem(digits[t] + j, radices[t])
        return digit, me + (digit - digits[t]) * strides[t]

    loads = [pltpu.make_async_copy(w_hbm, w, load_sem.at[0]),
             pltpu.make_async_copy(ups_hbm, ups, load_sem.at[1])]
    load_acts = pltpu.make_async_copy(acts_hbm, acts, load_sem.at[2])
    load_acts.start()
    for copy in loads:
        copy.start()

    barrier = pltpu.get_barrier_semaphore()
    partners = [left, right] + [peer(t, j)[1] for t in range(stages) for j in range(1, radices[t])]
    for partner in partners:
        pl.semaphore_signal(barrier, inc=1, device_id=(s, partner), device_id_type=MESH)

    @pl.when(s > 0)
    def _():
        pl.semaphore_signal(barrier, inc=1, device_id=(s - 1, me), device_id_type=MESH)

    @pl.when(s < sections - 1)
    def _():
        pl.semaphore_signal(barrier, inc=1, device_id=(s + 1, me), device_id_type=MESH)

    layers = jnp.where(s > 0, 1, 0) + jnp.where(s < sections - 1, 1, 0)
    pl.semaphore_wait(barrier, len(partners) + layers)

    def remote(src, dst, send, recv, where):
        return pltpu.make_async_remote_copy(
            src_ref=src, dst_ref=dst, send_sem=send, recv_sem=recv, device_id=where,
            device_id_type=MESH)

    first, last = pl.ds(0, HALO), pl.ds(rows - HALO, HALO)
    halos = [
        remote(acts_hbm.at[:, last], acts_lo, acts_send.at[0], acts_recv.at[0], (s, right)),
        remote(acts_hbm.at[:, first], acts_hi, acts_send.at[1], acts_recv.at[1], (s, left)),
        remote(nbr, nbr_lo, nbr_send.at[0], nbr_recv.at[0], (s, right)),
        remote(nbr, nbr_hi, nbr_send.at[1], nbr_recv.at[1], (s, left)),
    ]
    for copy in halos:
        copy.start()

    total = rows * count

    def counts(ids, shift, places):
        local = ids - me * rows + shift
        local = jnp.where(local < 0, local + total, local)
        local = jnp.where(local >= total, local - total, local)
        place = lax.broadcasted_iota(jnp.int32, (places, ids.shape[1]), 0)
        found = jnp.zeros(place.shape, F32)
        for k in range(K):
            found = found + jnp.where(local[k:k + 1] == place, 1.0, 0.0)
        return found

    gather = counts(nbr[...], HALO, span).T.astype(BF16)
    own = counts(nbr[...], 0, rows)
    load_acts.wait()
    for copy in halos[:2]:
        copy.wait_recv()

    for m in range(micro):
        field = jnp.concatenate([acts_lo[m], acts[m], acts_hi[m]], axis=0)
        agg = jnp.dot(gather, field, preferred_element_type=F32) * (1.0 / K)
        z[m * rows:(m + 1) * rows] = (acts[m].astype(F32) + agg).astype(BF16)
    for copy in loads:
        copy.wait()
    for copy in halos[2:]:
        copy.wait_recv()
    lane = lax.broadcasted_iota(jnp.int32, nbr.shape, 1)
    beside = jnp.where(lane < HALO, nbr_hi[...], nbr_lo[...])
    beside = counts(beside, 0, rows)
    inner = lax.broadcasted_iota(jnp.int32, beside.shape, 1)
    edge = jnp.logical_or(inner < HALO, inner >= rows - HALO)
    scatter = jnp.concatenate([own, jnp.where(edge, beside, 0.0)], axis=1).astype(BF16)
    blank = jnp.zeros((rows - 2 * HALO, chunk), BF16)

    def columns(c):
        return slice(c * chunk, (c + 1) * chunk)

    def factor(c):
        u = jnp.dot(z[...], w[:, columns(c)], preferred_element_type=F32)
        sig = jax.nn.sigmoid(u)
        return sig * (1.0 + u * (1.0 - sig))

    def turn():
        zt[...] = z[...].astype(F32).T.astype(BF16)

    def du_copies(c):
        return [
            remote(du.at[c, :, last], du_lo.at[c], du_send.at[2 * c], du_recv.at[2 * c], (s, right)),
            remote(du.at[c, :, first], du_hi.at[c], du_send.at[2 * c + 1], du_recv.at[2 * c + 1],
                   (s, left)),
        ]

    def put_du(c, value):
        value = value.astype(BF16)
        du[c] = value.reshape(micro, rows, chunk)
        for copy in du_copies(c):
            copy.start()

    def mix(c):
        for copy in du_copies(c):
            copy.wait_recv()
        for m in range(micro):
            field = jnp.concatenate([du[c, m], du_hi[c, m], blank, du_lo[c, m]], axis=0)
            spread = jnp.dot(scatter, field, preferred_element_type=F32) * (1.0 / K)
            e[m * rows:(m + 1) * rows, columns(c)] = (du[c, m].astype(F32) + spread).astype(BF16)

    def cotangent(c, g):
        value = g.astype(F32) + lax.dot_general(
            e[...], w[columns(c), :], (((1,), (1,)), ((), ())), preferred_element_type=F32)
        value = value.astype(BF16)
        out[:, columns(c)] = value
        return value

    def rs_copies(t, c):
        groups = parts[t].shape[1] // radices[t]
        base = sum(r - 1 for r in radices[:t]) * chunks + c * (radices[t] - 1)
        made = []
        for j in range(1, radices[t]):
            digit, partner = peer(t, j)
            made.append(remote(
                parts[t].at[c, pl.ds(digit * groups, groups)], landed[t].at[c, j - 1],
                rs_send.at[base + j - 1], rs_recv.at[base + j - 1], (s, partner)))
        return made

    def rs_start(t, c):
        for copy in rs_copies(t, c):
            copy.start()

    def weight_part(c):
        found = jnp.dot(zt[...], du[c].reshape(micro * rows, chunk), preferred_element_type=F32)
        found = found.astype(BF16)
        deep = width // count
        for piece in range(count):
            parts[0][c, position(piece, radices)] = found[piece * deep:(piece + 1) * deep]
        rs_start(0, c)

    def rs_step(t, c):
        for copy in rs_copies(t, c):
            copy.wait_recv()
        groups = parts[t].shape[1] // radices[t]
        value = parts[t][c, pl.ds(digits[t] * groups, groups)].astype(F32)
        for j in range(radices[t] - 1):
            value = value + landed[t][c, j].astype(F32)
        if t == stages - 1:
            wgrad[:, columns(c)] = value[0]
        else:
            parts[t + 1][c] = value.astype(BF16)
            rs_start(t + 1, c)

    def rs_wave(step):
        for t in reversed(range(stages)):
            if 0 <= step - t < chunks:
                rs_step(t, step - t)

    def g_copy(c):
        return remote(g_out.at[c], g_in.at[c], g_send.at[c], g_recv.at[c], (s - 1, me))

    @pl.when(top)
    def _():
        for c in range(chunks):
            put_du(c, ups[:, columns(c)].astype(F32) * factor(c))
        turn()
        for c in range(chunks):
            mix(c)
        for c in range(chunks):
            g_out[c] = cotangent(c, ups[:, columns(c)])
            if sections > 1:
                g_copy(c).start()
        for c in range(chunks):
            weight_part(c)
        for step in range(chunks + stages - 1):
            rs_wave(step)
        if sections > 1:
            for c in range(chunks):
                g_copy(c).wait_send()

    if sections > 1:
        @pl.when(jnp.logical_not(top))
        def _():
            for c in range(chunks):
                fac[:, columns(c)] = factor(c)
            turn()
            for c in range(chunks):
                g_copy(c).wait_recv()
                put_du(c, g_in[c].astype(F32) * fac[:, columns(c)])
                weight_part(c)
                for t in reversed(range(stages)):
                    if 0 <= c - t:
                        rs_step(t, c - t)
            for c in range(chunks):
                mix(c)
            for c in range(chunks):
                g_out[c] = cotangent(c, g_in[c])

                @pl.when(s > 0)
                def _():
                    g_copy(c).start()
            for step in range(chunks, chunks + stages - 1):
                rs_wave(step)

            @pl.when(s > 0)
            def _():
                for c in range(chunks):
                    g_copy(c).wait_send()

    for copy in halos:
        copy.wait_send()
    for c in range(chunks):
        for copy in du_copies(c):
            copy.wait_send()
        for t in range(stages):
            for copy in rs_copies(t, c):
                copy.wait_send()


def shards(sections, count, acts, upstream, weights, neighbours):
    micro, rows, width = upstream.shape
    chunk = min(CHUNK, width)
    chunks = width // chunk
    radices = radices_of(count)
    held, parts, landed = count, [], []
    deep = width // count
    for r in radices:
        parts.append(pltpu.VMEM((chunks, held, deep, chunk), BF16))
        held //= r
        landed.append(pltpu.VMEM((chunks, r - 1, held, deep, chunk), BF16))
    flights = sum(r - 1 for r in radices) * chunks
    dma = pltpu.SemaphoreType.DMA
    tall = micro * rows
    scratch = [
        pltpu.VMEM((width, width), BF16),
        pltpu.VMEM((tall, width), BF16),
        pltpu.VMEM((micro, rows, width), BF16),
        pltpu.VMEM((micro, HALO, width), BF16),
        pltpu.VMEM((micro, HALO, width), BF16),
        pltpu.VMEM((K, rows), jnp.int32),
        pltpu.VMEM((K, rows), jnp.int32),
        pltpu.VMEM((tall, width), BF16),
        pltpu.VMEM((width, tall), BF16),
        pltpu.VMEM((tall, width), F32),
        pltpu.VMEM((chunks, tall, chunk), BF16),
        pltpu.VMEM((chunks, tall, chunk), BF16),
        pltpu.VMEM((chunks, micro, rows, chunk), BF16),
        pltpu.VMEM((chunks, micro, HALO, chunk), BF16),
        pltpu.VMEM((chunks, micro, HALO, chunk), BF16),
        pltpu.VMEM((tall, width), BF16),
        dma((3,)), dma((2,)), dma((2,)), dma((2,)), dma((2,)), dma((chunks,)), dma((chunks,)),
        dma((2 * chunks,)), dma((2 * chunks,)), dma((flights,)), dma((flights,)),
    ] + parts + landed
    vmem = pl.BlockSpec(memory_space=pltpu.VMEM)
    grads, weight_grad = pl.pallas_call(
        functools.partial(kernel, sections, count, radices, chunk),
        out_shape=(
            jax.ShapeDtypeStruct((tall, width), BF16),
            jax.ShapeDtypeStruct((deep, width), F32),
        ),
        in_specs=[vmem, pl.BlockSpec(memory_space=pl.ANY), pl.BlockSpec(memory_space=pl.ANY), pl.BlockSpec(memory_space=pl.ANY)],
        out_specs=(vmem, vmem),
        scratch_shapes=scratch,
        compiler_params=pltpu.CompilerParams(
            collective_id=0, has_side_effects=True, vmem_limit_bytes=60 * 1024 * 1024),
    )(neighbours.T, acts[0], upstream.reshape(tall, width), weights[0])
    return grads.reshape(1, micro, rows, width), weight_grad[None]


def solution(mesh):
    in_specs = (
        P("section", None, "space", None),
        P(None, "space", None),
        P("section", None, None),
        P("space", None),
    )
    out_specs = (P("section", None, "space", None), P("section", "space", None))
    body = functools.partial(shards, mesh.shape["section"], mesh.shape["space"])
    return jax.shard_map(
        body, mesh=mesh, in_specs=in_specs, out_specs=out_specs, check_vma=False)
```

```python
import functools

import jax
import jax.numpy as jnp
from jax import lax
from jax.experimental import pallas as pl
from jax.experimental.pallas import tpu as pltpu
from jax.sharding import PartitionSpec as P

K = 6
HALO = 32
CHUNK = 256
MESH = pl.DeviceIdType.MESH
F32 = jnp.float32
BF16 = jnp.bfloat16


def radices_of(count):
    found = []
    for _ in range(2):
        if count % 2 == 0:
            found.append(2)
            count //= 2
    while count > 1:
        factor = next(f for f in (4, 2, 3, 5, 7, count) if count % f == 0)
        found.append(factor)
        count //= factor
    return tuple(found)


def position(piece, radices):
    left = 1
    for r in radices:
        left *= r
    place = 0
    for r in radices:
        left //= r
        place += (piece % r) * left
        piece //= r
    return place


def kernel(sections, count, radices, chunk, nbr, acts_hbm, ups_hbm, w_hbm, out, wgrad, *scratch):
    (w, ups, acts, acts_lo, acts_hi, nbr_lo, nbr_hi, z, zt, fac, g_in, g_out, du, du_lo, du_hi, e,
     load_sem, acts_send, acts_recv, nbr_send, nbr_recv, g_send, g_recv, du_send, du_recv,
     rs_send, rs_recv, *rs) = scratch
    stages = len(radices)
    parts, landed = rs[:stages], rs[stages:]
    micro, rows, width = acts.shape
    chunks = width // chunk
    span = rows + 2 * HALO
    s = lax.axis_index("section")
    me = lax.axis_index("space")
    right, left = lax.rem(me + 1, count), lax.rem(me + count - 1, count)
    top = s == sections - 1

    strides, digits, stride = [], [], 1
    for r in radices:
        strides.append(stride)
        digits.append(lax.rem(lax.div(me, stride), r))
        stride *= r

    def peer(t, j):
        digit = lax.rem(digits[t] + j, radices[t])
        return digit, me + (digit - digits[t]) * strides[t]

    loads = [pltpu.make_async_copy(w_hbm, w, load_sem.at[0]),
             pltpu.make_async_copy(ups_hbm, ups, load_sem.at[1])]
    load_acts = pltpu.make_async_copy(acts_hbm, acts, load_sem.at[2])
    load_acts.start()
    for copy in loads:
        copy.start()

    barrier = pltpu.get_barrier_semaphore()
    partners = [left, right] + [peer(t, j)[1] for t in range(stages) for j in range(1, radices[t])]
    for partner in partners:
        pl.semaphore_signal(barrier, inc=1, device_id=(s, partner), device_id_type=MESH)

    @pl.when(s > 0)
    def _():
        pl.semaphore_signal(barrier, inc=1, device_id=(s - 1, me), device_id_type=MESH)

    @pl.when(s < sections - 1)
    def _():
        pl.semaphore_signal(barrier, inc=1, device_id=(s + 1, me), device_id_type=MESH)

    layers = jnp.where(s > 0, 1, 0) + jnp.where(s < sections - 1, 1, 0)
    pl.semaphore_wait(barrier, len(partners) + layers)

    def remote(src, dst, send, recv, where):
        return pltpu.make_async_remote_copy(
            src_ref=src, dst_ref=dst, send_sem=send, recv_sem=recv, device_id=where,
            device_id_type=MESH)

    first, last = pl.ds(0, HALO), pl.ds(rows - HALO, HALO)
    halos = [
        remote(acts_hbm.at[:, last], acts_lo, acts_send.at[0], acts_recv.at[0], (s, right)),
        remote(acts_hbm.at[:, first], acts_hi, acts_send.at[1], acts_recv.at[1], (s, left)),
        remote(nbr, nbr_lo, nbr_send.at[0], nbr_recv.at[0], (s, right)),
        remote(nbr, nbr_hi, nbr_send.at[1], nbr_recv.at[1], (s, left)),
    ]
    for copy in halos:
        copy.start()

    total = rows * count

    def counts(ids, shift, places):
        local = ids - me * rows + shift
        local = jnp.where(local < 0, local + total, local)
        local = jnp.where(local >= total, local - total, local)
        place = lax.broadcasted_iota(jnp.int32, (places, ids.shape[1]), 0)
        found = jnp.zeros(place.shape, F32)
        for k in range(K):
            found = found + jnp.where(local[k:k + 1] == place, 1.0, 0.0)
        return found

    gather = counts(nbr[...], HALO, span).T.astype(BF16)
    own = counts(nbr[...], 0, rows)
    load_acts.wait()
    for copy in halos[:2]:
        copy.wait_recv()

    for m in range(micro):
        field = jnp.concatenate([acts_lo[m], acts[m], acts_hi[m]], axis=0)
        agg = jnp.dot(gather, field, preferred_element_type=F32) * (1.0 / K)
        z[m * rows:(m + 1) * rows] = (acts[m].astype(F32) + agg).astype(BF16)
    for copy in loads:
        copy.wait()
    for copy in halos[2:]:
        copy.wait_recv()
    lane = lax.broadcasted_iota(jnp.int32, nbr.shape, 1)
    beside = jnp.where(lane < HALO, nbr_hi[...], nbr_lo[...])
    beside = counts(beside, 0, rows)
    inner = lax.broadcasted_iota(jnp.int32, beside.shape, 1)
    edge = jnp.logical_or(inner < HALO, inner >= rows - HALO)
    scatter = jnp.concatenate([own, jnp.where(edge, beside, 0.0)], axis=1).astype(BF16)
    blank = jnp.zeros((rows - 2 * HALO, chunk), BF16)

    def columns(c):
        return slice(c * chunk, (c + 1) * chunk)

    def factor(c):
        u = jnp.dot(z[...], w[:, columns(c)], preferred_element_type=F32)
        sig = jax.nn.sigmoid(u)
        return sig * (1.0 + u * (1.0 - sig))

    def turn():
        zt[...] = z[...].astype(F32).T.astype(BF16)

    def du_copies(c):
        return [
            remote(du.at[c, :, last], du_lo.at[c], du_send.at[2 * c], du_recv.at[2 * c], (s, right)),
            remote(du.at[c, :, first], du_hi.at[c], du_send.at[2 * c + 1], du_recv.at[2 * c + 1],
                   (s, left)),
        ]

    def put_du(c, value):
        value = value.astype(BF16)
        du[c] = value.reshape(micro, rows, chunk)
        for copy in du_copies(c):
            copy.start()

    def mix(c):
        for copy in du_copies(c):
            copy.wait_recv()
        for m in range(micro):
            field = jnp.concatenate([du[c, m], du_hi[c, m], blank, du_lo[c, m]], axis=0)
            spread = jnp.dot(scatter, field, preferred_element_type=F32) * (1.0 / K)
            e[m * rows:(m + 1) * rows, columns(c)] = (du[c, m].astype(F32) + spread).astype(BF16)

    def cotangent(c, g):
        value = g.astype(F32) + lax.dot_general(
            e[...], w[columns(c), :], (((1,), (1,)), ((), ())), preferred_element_type=F32)
        value = value.astype(BF16)
        out[:, columns(c)] = value
        return value

    def rs_copies(t, c):
        groups = parts[t].shape[1] // radices[t]
        base = sum(r - 1 for r in radices[:t]) * chunks + c * (radices[t] - 1)
        made = []
        for j in range(1, radices[t]):
            digit, partner = peer(t, j)
            made.append(remote(
                parts[t].at[c, pl.ds(digit * groups, groups)], landed[t].at[c, j - 1],
                rs_send.at[base + j - 1], rs_recv.at[base + j - 1], (s, partner)))
        return made

    def rs_start(t, c):
        for copy in rs_copies(t, c):
            copy.start()

    def weight_part(c):
        found = jnp.dot(zt[...], du[c].reshape(micro * rows, chunk), preferred_element_type=F32)
        found = found.astype(BF16)
        deep = width // count
        for piece in range(count):
            parts[0][c, position(piece, radices)] = found[piece * deep:(piece + 1) * deep]
        rs_start(0, c)

    def rs_step(t, c):
        for copy in rs_copies(t, c):
            copy.wait_recv()
        groups = parts[t].shape[1] // radices[t]
        value = parts[t][c, pl.ds(digits[t] * groups, groups)].astype(F32)
        for j in range(radices[t] - 1):
            value = value + landed[t][c, j].astype(F32)
        if t == stages - 1:
            wgrad[:, columns(c)] = value[0]
        else:
            parts[t + 1][c] = value.astype(BF16)
            rs_start(t + 1, c)

    def rs_wave(step):
        for t in reversed(range(stages)):
            if 0 <= step - t < chunks:
                rs_step(t, step - t)

    def g_copy(c):
        return remote(g_out.at[c], g_in.at[c], g_send.at[c], g_recv.at[c], (s - 1, me))

    @pl.when(top)
    def _():
        for c in range(chunks):
            put_du(c, ups[:, columns(c)].astype(F32) * factor(c))
        turn()
        for c in range(chunks):
            mix(c)
        for c in range(chunks):
            g_out[c] = cotangent(c, ups[:, columns(c)])
            if sections > 1:
                g_copy(c).start()
        for c in range(chunks):
            weight_part(c)
        for step in range(chunks + stages - 1):
            rs_wave(step)
        if sections > 1:
            for c in range(chunks):
                g_copy(c).wait_send()

    if sections > 1:
        @pl.when(jnp.logical_not(top))
        def _():
            for c in range(chunks):
                fac[:, columns(c)] = factor(c)
            turn()
            for c in range(chunks):
                g_copy(c).wait_recv()
                put_du(c, g_in[c].astype(F32) * fac[:, columns(c)])
                weight_part(c)
                for t in range(min(stages, c + 1)):
                    rs_step(t, c - t)
            for c in range(chunks):
                mix(c)
            for c in range(chunks):
                g_out[c] = cotangent(c, g_in[c])

                @pl.when(s > 0)
                def _():
                    g_copy(c).start()
            for step in range(chunks, chunks + stages - 1):
                rs_wave(step)

            @pl.when(s > 0)
            def _():
                for c in range(chunks):
                    g_copy(c).wait_send()

    for copy in halos:
        copy.wait_send()
    for c in range(chunks):
        for copy in du_copies(c):
            copy.wait_send()
        for t in range(stages):
            for copy in rs_copies(t, c):
                copy.wait_send()


def shards(sections, count, acts, upstream, weights, neighbours):
    micro, rows, width = upstream.shape
    chunk = min(CHUNK, width)
    chunks = width // chunk
    radices = radices_of(count)
    held, parts, landed = count, [], []
    deep = width // count
    for r in radices:
        parts.append(pltpu.VMEM((chunks, held, deep, chunk), BF16))
        held //= r
        landed.append(pltpu.VMEM((chunks, r - 1, held, deep, chunk), BF16))
    flights = sum(r - 1 for r in radices) * chunks
    dma = pltpu.SemaphoreType.DMA
    tall = micro * rows
    scratch = [
        pltpu.VMEM((width, width), BF16),
        pltpu.VMEM((tall, width), BF16),
        pltpu.VMEM((micro, rows, width), BF16),
        pltpu.VMEM((micro, HALO, width), BF16),
        pltpu.VMEM((micro, HALO, width), BF16),
        pltpu.VMEM((K, rows), jnp.int32),
        pltpu.VMEM((K, rows), jnp.int32),
        pltpu.VMEM((tall, width), BF16),
        pltpu.VMEM((width, tall), BF16),
        pltpu.VMEM((tall, width), F32),
        pltpu.VMEM((chunks, tall, chunk), BF16),
        pltpu.VMEM((chunks, tall, chunk), BF16),
        pltpu.VMEM((chunks, micro, rows, chunk), BF16),
        pltpu.VMEM((chunks, micro, HALO, chunk), BF16),
        pltpu.VMEM((chunks, micro, HALO, chunk), BF16),
        pltpu.VMEM((tall, width), BF16),
        dma((3,)), dma((2,)), dma((2,)), dma((2,)), dma((2,)), dma((chunks,)), dma((chunks,)),
        dma((2 * chunks,)), dma((2 * chunks,)), dma((flights,)), dma((flights,)),
    ] + parts + landed
    vmem = pl.BlockSpec(memory_space=pltpu.VMEM)
    grads, weight_grad = pl.pallas_call(
        functools.partial(kernel, sections, count, radices, chunk),
        out_shape=(
            jax.ShapeDtypeStruct((tall, width), BF16),
            jax.ShapeDtypeStruct((deep, width), F32),
        ),
        in_specs=[vmem, pl.BlockSpec(memory_space=pl.ANY), pl.BlockSpec(memory_space=pl.ANY), pl.BlockSpec(memory_space=pl.ANY)],
        out_specs=(vmem, vmem),
        scratch_shapes=scratch,
        compiler_params=pltpu.CompilerParams(
            collective_id=0, has_side_effects=True, vmem_limit_bytes=60 * 1024 * 1024),
    )(neighbours.T, acts[0], upstream.reshape(tall, width), weights[0])
    return grads.reshape(1, micro, rows, width), weight_grad[None]


def solution(mesh):
    in_specs = (
        P("section", None, "space", None),
        P(None, "space", None),
        P("section", None, None),
        P("space", None),
    )
    out_specs = (P("section", None, "space", None), P("section", "space", None))
    body = functools.partial(shards, mesh.shape["section"], mesh.shape["space"])
    return jax.shard_map(
        body, mesh=mesh, in_specs=in_specs, out_specs=out_specs, check_vma=False)
```
